32 devices in a mesh: gx: 4 (over y, core), gy: 8 (over z, x).
Axes of the slice: x: 2, y: 2, z: 4, core: 2. Of those that a mesh axis runs over, the one named last changes fastest.
Arguments:
- table: bfloat16 [8192, 128], P(('gx', 'gy')), may hold values from -6 to 6
- request_rows: int32 [32, 32, 32], P(('gx', 'gy')), may hold values from 0 to 255, as said below
- send_counts: int32 [32, 32], P(('gx', 'gy')), may hold values from 1 to 32, as said below
- lookup_owner: int32 [131072], P(('gx', 'gy')), may hold values from 0 to 31
- lookup_rank: int32 [131072], P(('gx', 'gy')), may hold values from 0 to 31
- bag_lengths: int32 [32, 2048], P(('gx', 'gy')), may hold values from 1 to 8, 4096 in all within a row
- labels: int32 [4096], P(('gx', 'gy')), may hold values 0 or 1
- w_first: bfloat16 [2048, 2048], replicated, may hold values from -0.125 to 0.125
- w_second: bfloat16 [2048, 2048], replicated, may hold values from -0.125 to 0.125
- w_out: bfloat16 [2048], replicated, may hold values from -0.625 to 0.625
Outputs:
- grad_first: float32 [2048, 2048], P(('gx', 'gy'))
- grad_second: float32 [2048, 2048], P(('gx', 'gy'))
- grad_out: float32 [2048], P(('gx', 'gy'))
- row_grad: float32 [8192, 128], P(('gx', 'gy'))
The draws below stay inside these ranges and needn't reach their ends.
Inputs may be any that keep to these rules, and one draw needn't show every extreme that they name: `request_rows`: the 32 local rows of one trainer and one owner are distinct. `send_counts`: each trainer sends 32 live slots to at least one owner.
All inputs are finite; a program needn't handle non-finite values. No bound on the sum of `labels` on one device may be relied on, other than what follows from the above.
Results may differ from the reference program's by a relative error of at most 0.009.
Values may be sent and summed in bfloat16 or wider, within the bound.
A program may use at most 128 MiB of HBM per device.

```python
import math
import jax
import jax.numpy as jnp
import numpy as np
from jax import lax

EMB = 128
HID = 2048
ROWS_DEV = 256
CAP = 32
MOST = 8
INPUT = 2048
BAGS_DEV = 2048
LOOK_DEV = 4096
LOOKUPS = 131072
SAMPLES = 4096
ROWS = 8192
DEVICES = 32


def draw_request_rows(key, part):
    key = jax.random.fold_in(key, 11)
    first, second = jax.random.split(key)
    begin = jax.random.randint(first, (DEVICES, DEVICES, 1), 0, ROWS_DEV)
    stride = 2 * jax.random.randint(second, (DEVICES, DEVICES, 1), 0, ROWS_DEV // 2) + 1
    steps = jnp.arange(CAP, dtype=jnp.int32)[None, None, :]
    return ((begin + stride * steps) % ROWS_DEV).astype(jnp.int32)


def draw_send_counts(key, part):
    key = jax.random.fold_in(key, 12)
    first, second = jax.random.split(key)
    counts = jax.random.randint(first, (DEVICES, DEVICES), 1, CAP + 1)
    full = jax.random.randint(second, (DEVICES, 1), 0, DEVICES)
    column = jnp.arange(DEVICES, dtype=jnp.int32)[None, :]
    return jnp.where(column == full, CAP, counts).astype(jnp.int32)


def place_ends(result, key, low, high):
    extent = result.shape
    index_at = [jax.random.randint(jax.random.fold_in(key, axis), (), 0, extent[axis]) for axis in range(len(extent))]
    result = result.at[tuple(index_at)].set(low)
    longest = extent.index(max(extent))
    index_at[longest] = (index_at[longest] + 1) % extent[longest]
    return result.at[tuple(index_at)].set(high)


def block_levels(rng, shape, shards, least, largest):
    level = 1.0
    for dim, shards_of in shards:
        draws = jax.random.uniform(jax.random.fold_in(jax.random.fold_in(rng, 6), dim), (shards_of,), jnp.float32, least / len(shards), largest / len(shards))
        level = level * jnp.repeat(jnp.exp(draws), shape[dim] // shards_of).reshape((-1,) + (1,) * (len(shape) - 1 - dim))
    return level


def rank_table(number_of, skew):
    portions = [(1 << 20) // math.isqrt(rank ** skew) + 1 for rank in range(1, number_of + 1)]
    spread = 1 + sum(portions) // (1 << 30)
    return np.cumsum(np.array([max(1, weight // spread) for weight in portions]))


def skewed_ids(rng, shape, count, slope):
    listing = rank_table(count, slope)
    ticket = jax.random.randint(jax.random.fold_in(rng, 1), shape, 0, int(listing[count - 1]))
    grade = jnp.searchsorted(jnp.asarray(listing, jnp.int32), ticket, side="right")
    return jax.random.permutation(jax.random.fold_in(rng, 2), count)[grade].astype(jnp.int32)


def split_up(amount, total, bound, lean):
    weights = [(1 << 20) // math.isqrt(standing ** lean) + 1 for standing in range(2, amount + 1)]
    rest, given = total - bound - (amount - 1), [1] * (amount - 1)
    while rest > 0:
        free = [i for i in range(amount - 1) if given[i] < bound]
        whole, remaining = sum([weights[i] for i in free]), rest
        for i in free:
            addition = min(bound - given[i], max(1, remaining * weights[i] // whole), rest)
            given[i] = given[i] + addition
            rest = rest - addition
    return np.array([bound] + given)


def ragged_sizes(stream_key, number_of, total, most, lean):
    if number_of == 2:
        one = jax.random.randint(stream_key, (), max(1, total - most), min(most, total - 1) + 1)
        return jnp.stack([one, total - one])
    tallies = jnp.asarray(split_up(number_of, total, most, lean), jnp.int32)
    couples = (number_of - 1) // 2
    donor, sink = tallies[1:1 + 2 * couples:2], tallies[2:2 + 2 * couples:2]
    margin = jnp.minimum(donor - 1, most - sink)
    moved = jax.random.randint(jax.random.fold_in(stream_key, 1), (couples,), 0, 1 << 20) % (margin + 1)
    tallies = tallies.at[1:1 + 2 * couples:2].set(donor - moved).at[2:2 + 2 * couples:2].set(sink + moved)
    return tallies[jax.random.permutation(jax.random.fold_in(stream_key, 2), number_of)]


def centred(own_key, extent, spread, reach, shards=(), kind=jnp.bfloat16):
    level = block_levels(own_key, extent, shards, -0.22, 0.18) if shards else 1.0
    drawn = jax.random.normal(own_key, extent, jnp.float32) * spread * level
    return jnp.minimum(jnp.maximum(drawn, -reach), reach).astype(kind)


def setup_inputs(seed: int = 0) -> dict:
    key_of = jax.random.split(jax.random.key(seed), 11)
    table = centred(key_of[0], (ROWS, EMB), 1.0, 6.0, ((0, 32),))
    request_rows = draw_request_rows(jax.random.fold_in(key_of[10], 71), 0)
    send_counts = draw_send_counts(jax.random.fold_in(key_of[10], 71), 0)
    lookup_owner = place_ends(skewed_ids(key_of[3], (LOOKUPS,), DEVICES, 2), jax.random.fold_in(key_of[3], 3), 0, DEVICES - 1).astype(jnp.int32)
    lookup_rank = place_ends(jax.random.randint(key_of[4], (LOOKUPS,), 0, CAP), jax.random.fold_in(key_of[4], 1), 0, CAP - 1).astype(jnp.int32)
    bag_lengths = jax.vmap(lambda own: ragged_sizes(own, BAGS_DEV, LOOK_DEV, MOST, 2))(jax.random.split(key_of[5], DEVICES)).reshape((DEVICES, BAGS_DEV)).astype(jnp.int32)
    labels = place_ends((jax.random.randint(key_of[6], (SAMPLES,), 0, 2) < 1).astype(jnp.int32), jax.random.fold_in(key_of[6], 1), 0, 1)
    w_first = centred(key_of[7], (INPUT, HID), INPUT ** -0.5, 0.125)
    w_second = centred(key_of[8], (HID, HID), HID ** -0.5, 0.125)
    w_out = centred(key_of[9], (HID,), 100 ** -0.5, 0.625)
    return {"table": table, "request_rows": request_rows, "send_counts": send_counts, "lookup_owner": lookup_owner, "lookup_rank": lookup_rank, "bag_lengths": bag_lengths, "labels": labels, "w_first": w_first, "w_second": w_second, "w_out": w_out}


def silu_slope(value):
    sig = jax.nn.sigmoid(value)
    return sig * (1.0 + value * (1.0 - sig))

def reference(table, request_rows, send_counts, lookup_owner, lookup_rank, bag_lengths, labels, w_first, w_second, w_out):
    owner = lookup_owner.reshape(DEVICES, LOOK_DEV).astype(jnp.int32)
    rank = lookup_rank.reshape(DEVICES, LOOK_DEV).astype(jnp.int32)
    trainer = jnp.arange(DEVICES, dtype=jnp.int32)[:, None]
    count = send_counts[trainer, owner]
    local = request_rows[trainer, owner, rank % count]
    gid = (owner * ROWS_DEV + local).astype(jnp.int32).reshape(-1)
    lengths = bag_lengths.astype(jnp.int32)
    starts = jnp.cumsum(lengths, axis=1) - lengths
    marks = jnp.zeros((DEVICES, LOOK_DEV), jnp.int32).at[trainer, starts].add(1)
    bag_of = jnp.cumsum(marks, axis=1) - 1
    bag = (trainer * BAGS_DEV + bag_of).astype(jnp.int32).reshape(-1)
    scale = lax.rsqrt(lengths.reshape(-1).astype(jnp.float32))[:, None]
    rows = table[gid].astype(jnp.float32)
    pooled = jax.ops.segment_sum(rows, bag, num_segments=DEVICES * BAGS_DEV) * scale
    x = pooled.reshape(SAMPLES, INPUT).astype(jnp.bfloat16)
    z1 = jnp.dot(x, w_first, preferred_element_type=jnp.float32)
    h1 = jax.nn.silu(z1).astype(jnp.bfloat16)
    z2 = jnp.dot(h1, w_second, preferred_element_type=jnp.float32)
    h2 = jax.nn.silu(z2).astype(jnp.bfloat16)
    logit = jnp.dot(h2, w_out, preferred_element_type=jnp.float32)
    dlogit = jax.nn.sigmoid(logit) - labels.astype(jnp.float32)
    dz2 = (dlogit[:, None] * w_out.astype(jnp.float32)[None, :] * silu_slope(z2)).astype(jnp.bfloat16)
    grad_out = jnp.dot(dlogit, h2.astype(jnp.float32), precision=lax.Precision.HIGHEST)
    grad_second = jnp.dot(h1.T, dz2, preferred_element_type=jnp.float32)
    back_two = lax.dot_general(dz2, w_second, (((1,), (1,)), ((), ())), preferred_element_type=jnp.float32)
    dz1 = (back_two * silu_slope(z1)).astype(jnp.bfloat16)
    grad_first = jnp.dot(x.T, dz1, preferred_element_type=jnp.float32)
    back_one = lax.dot_general(dz1, w_first, (((1,), (1,)), ((), ())), preferred_element_type=jnp.float32)
    bag_grad = (back_one.reshape(DEVICES * BAGS_DEV, EMB) * scale).astype(jnp.bfloat16)
    lookup_grad = bag_grad[bag].astype(jnp.float32)
    row_grad = jax.ops.segment_sum(lookup_grad, gid, num_segments=ROWS)
    return (grad_first, grad_second, grad_out, row_grad)
```

```python
import jax
import jax.numpy as jnp
from jax import lax
from jax.sharding import PartitionSpec as P

AXES = ("gx", "gy")


def silu_slope(value):
    sig = jax.nn.sigmoid(value)
    return sig * (1.0 + value * (1.0 - sig))


def swap(value, mask):
    peers = lax.axis_size(AXES)
    return lax.ppermute(value, AXES, [(d, d ^ mask) for d in range(peers)])


def pick(value, dim, index):
    return lax.dynamic_index_in_dim(value, index, dim, keepdims=False)


def gather_left(left, core_bit):
    peers = lax.axis_size(AXES)
    me = lax.axis_index(AXES)
    samples, total = left.shape
    core, low = (me >> core_bit) & 1, me & 1
    split = left.T.reshape(
        peers >> (core_bit + 1), 2, 1 << (core_bit - 1), 2, total // peers, samples
    )

    def quarter(c, x):
        return pick(pick(split, 3, x), 1, c)

    return jnp.concatenate(
        [
            quarter(core, low),
            swap(quarter(1 - core, low), 1 << core_bit),
            swap(quarter(core, 1 - low), 1),
            swap(quarter(1 - core, 1 - low), 1 + (1 << core_bit)),
        ],
        axis=-1,
    )


def reduce_gradient(left, right, core_bit):
    peers = lax.axis_size(AXES)
    me = lax.axis_index(AXES)
    across = swap(right, 1)
    right = jnp.concatenate(
        [right, swap(right, 1 << core_bit), across, swap(across, 1 << core_bit)], axis=0
    )
    high = [b for b in range(peers.bit_length() - 2, core_bit, -1)]
    mid = [b for b in range(core_bit - 1, 0, -1)]
    bits = high + mid
    rows, depth = left.shape[-2:]
    left = left.reshape([2] * len(bits) + [rows, depth])

    def product(part):
        out = jnp.dot(part.reshape(-1, depth), right, preferred_element_type=jnp.float32)
        return out.reshape(part.shape[:-1] + (right.shape[1],))

    current = None
    for bit in high[::-1] + mid[::-1]:
        dim = bits.index(bit)
        mine = (me >> bit) & 1
        if current is None:
            sent = product(pick(left, dim, 1 - mine)).astype(jnp.bfloat16)
            got = swap(sent, 1 << bit)
            kept = product(pick(left, dim, mine))
        else:
            got = swap(pick(current, dim, 1 - mine).astype(jnp.bfloat16), 1 << bit)
            kept = pick(current, dim, mine)
        current = kept + got.astype(jnp.float32)
        bits.remove(bit)
    return current.reshape(rows, -1)


def per_device(
    table,
    request_rows,
    send_counts,
    lookup_owner,
    lookup_rank,
    bag_lengths,
    labels,
    w_first,
    w_second,
    w_out,
):
    peers = lax.axis_size(AXES)
    core_bit = lax.axis_size("gy").bit_length() - 1
    slots = request_rows.shape[2]
    width = table.shape[1]
    looks = lookup_owner.shape[0]
    samples = labels.shape[0]
    bags = bag_lengths.shape[1]
    inputs = w_first.shape[0]
    most = 8
    incoming = lax.all_to_all(
        request_rows, AXES, split_axis=1, concat_axis=0, tiled=True
    ).reshape(peers * slots)
    served = table[incoming]
    fetched = lax.all_to_all(
        served.reshape(peers, 1, slots, width), AXES, split_axis=0, concat_axis=1, tiled=True
    ).reshape(peers * slots, width)

    owner_ids = jnp.arange(peers, dtype=jnp.int32)
    match = lookup_owner[:, None] == owner_ids[None, :]
    lookup_count = jnp.sum(jnp.where(match, send_counts[0][None, :], 0), axis=1)
    slot = lookup_rank % lookup_count
    lengths = bag_lengths[0]
    starts = jnp.cumsum(lengths) - lengths
    scale = lax.rsqrt(lengths.astype(jnp.float32))[:, None]
    owner_pad = jnp.pad(lookup_owner, (0, most)).astype(jnp.bfloat16)
    slot_pad = jnp.pad(slot, (0, most)).astype(jnp.bfloat16)
    shifted = jnp.stack(
        [owner_pad[j : j + looks] for j in range(most)]
        + [slot_pad[j : j + looks] for j in range(most)]
    )
    first = (starts[:, None] == jnp.arange(looks, dtype=jnp.int32)[None, :]).astype(jnp.bfloat16)
    found = lax.dot_general(
        first, shifted, (((1,), (1,)), ((), ())), preferred_element_type=jnp.float32
    )
    code = found[:, :most] * slots + found[:, most:]
    place = jnp.arange(most, dtype=jnp.int32)[None, :]
    code = jnp.where(place < lengths[:, None], code, -1.0)
    names = jnp.arange(peers * slots, dtype=jnp.int32).astype(jnp.float32)[None, :]
    counted = jnp.zeros((bags, peers * slots), jnp.float32)
    for j in range(most):
        counted = counted + (code[:, j : j + 1] == names).astype(jnp.float32)
    counted = counted.astype(jnp.bfloat16)

    pooled = jnp.dot(counted, fetched, preferred_element_type=jnp.float32)
    x = (pooled * scale).astype(jnp.bfloat16).reshape(samples, inputs)
    x_left = gather_left(x, core_bit)
    z1 = jnp.dot(x, w_first, preferred_element_type=jnp.float32)
    h1 = jax.nn.silu(z1).astype(jnp.bfloat16)
    h1_left = gather_left(h1, core_bit)
    z2 = jnp.dot(h1, w_second, preferred_element_type=jnp.float32)
    h2 = jax.nn.silu(z2).astype(jnp.bfloat16)
    logit = jnp.dot(h2, w_out, preferred_element_type=jnp.float32)
    dlogit = jax.nn.sigmoid(logit) - labels.astype(jnp.float32)
    dz2 = (dlogit[:, None] * w_out.astype(jnp.float32)[None, :] * silu_slope(z2)).astype(
        jnp.bfloat16
    )
    head_term = jnp.sum(dlogit[:, None] * h2.astype(jnp.float32), axis=0)
    grad_second = reduce_gradient(h1_left, dz2, core_bit)
    back_two = lax.dot_general(
        dz2, w_second, (((1,), (1,)), ((), ())), preferred_element_type=jnp.float32
    )
    dz1 = (back_two * silu_slope(z1)).astype(jnp.bfloat16)
    grad_first = reduce_gradient(x_left, dz1, core_bit)
    back_one = lax.dot_general(
        dz1, w_first, (((1,), (1,)), ((), ())), preferred_element_type=jnp.float32
    )
    bag_grad = (back_one.reshape(bags, width) * scale).astype(jnp.bfloat16)
    slot_grad = lax.dot_general(
        counted, bag_grad, (((0,), (0,)), ((), ())), preferred_element_type=jnp.float32
    )
    share = head_term.shape[0] // peers
    extra = -(-share // width)
    head = jnp.pad(head_term.reshape(peers, share), ((0, 0), (0, extra * width - share)))
    outgoing = jnp.concatenate(
        [slot_grad.reshape(peers, slots, width), head.reshape(peers, extra, width)], axis=1
    ).astype(jnp.bfloat16)
    returned = lax.all_to_all(outgoing[None], AXES, split_axis=1, concat_axis=0, tiled=True)[:, 0]
    grad_out = jnp.sum(returned[:, slots:].astype(jnp.float32), axis=0).reshape(-1)[:share]
    home = (
        jnp.arange(table.shape[0], dtype=jnp.int32)[:, None] == incoming[None, :]
    ).astype(jnp.bfloat16)
    row_grad = jnp.dot(
        home, returned[:, :slots].reshape(peers * slots, width), preferred_element_type=jnp.float32
    )
    return (grad_first, grad_second, grad_out, row_grad)


def solution(mesh):
    in_specs = (
        P(AXES, None),
        P(AXES, None, None),
        P(AXES, None),
        P(AXES),
        P(AXES),
        P(AXES, None),
        P(AXES),
        P(),
        P(),
        P(),
    )
    out_specs = (P(AXES, None), P(AXES, None), P(AXES), P(AXES, None))
    return jax.shard_map(
        per_device, mesh=mesh, in_specs=in_specs, out_specs=out_specs, check_vma=False
    )
```

```python
import jax
import jax.numpy as jnp
from jax import lax
from jax.sharding import PartitionSpec as P

AXES = ("gx", "gy")


def silu_slope(value):
    sig = jax.nn.sigmoid(value)
    return sig * (1.0 + value * (1.0 - sig))


def swap(value, mask):
    peers = lax.axis_size(AXES)
    return lax.ppermute(value, AXES, [(d, d ^ mask) for d in range(peers)])


def pick(value, dim, index):
    return lax.dynamic_index_in_dim(value, index, dim, keepdims=False)


def group(core_bit, side):
    core, near = 1 << core_bit, 1 << side
    return core, near, (lax.axis_index(AXES) >> core_bit) & 1, (lax.axis_index(AXES) >> side) & 1


def gather_left(left, core_bit, side):
    peers = lax.axis_size(AXES)
    core, near, my_core, my_near = group(core_bit, side)
    samples, total = left.shape
    bits = peers.bit_length() - 1
    one, two = bits - 1 - max(core_bit, side), bits - 1 - min(core_bit, side)
    split = left.T.reshape(
        1 << one, 2, 1 << (two - one - 1), 2, 1 << (bits - 1 - two), total // peers, samples
    )

    def quarter(c, n):
        outer, inner = (c, n) if core_bit > side else (n, c)
        return pick(pick(split, 3, inner), 1, outer)

    return jnp.concatenate(
        [
            quarter(my_core, my_near),
            swap(quarter(1 - my_core, my_near), core),
            swap(quarter(my_core, 1 - my_near), near),
            swap(quarter(1 - my_core, 1 - my_near), core + near),
        ],
        axis=-1,
    )


def gather_right(right, core_bit, side):
    core, near, _, _ = group(core_bit, side)
    across = swap(right, near)
    return jnp.concatenate([right, swap(right, core), across, swap(across, core)], axis=0)


def halving(left, right, core_bit, side):
    peers = lax.axis_size(AXES)
    me = lax.axis_index(AXES)
    bits = [b for b in range(peers.bit_length() - 2, -1, -1) if b not in (core_bit, side)]
    order = [b for b in (0,) + tuple(range(core_bit + 1, peers.bit_length() - 1)) if b in bits]
    order = order + [b for b in bits[::-1] if b not in order]
    rows, depth = left.shape[-2:]
    left = left.reshape([2] * len(bits) + [rows, depth])

    def product(part):
        out = jnp.dot(part.reshape(-1, depth), right, preferred_element_type=jnp.float32)
        return out.reshape(part.shape[:-1] + (right.shape[1],))

    dim = bits.index(order[0])
    mine = (me >> order[0]) & 1
    sent = product(pick(left, dim, 1 - mine)).astype(jnp.bfloat16)

    def rest(sent):
        left_bits = list(bits)
        current = None
        for bit in order:
            dim = left_bits.index(bit)
            mine = (me >> bit) & 1
            if current is None:
                got = swap(sent, 1 << bit)
                kept = product(pick(left, dim, mine))
            else:
                got = swap(pick(current, dim, 1 - mine).astype(jnp.bfloat16), 1 << bit)
                kept = pick(current, dim, mine)
            current = kept + got.astype(jnp.float32)
            left_bits.remove(bit)
        return current.reshape(rows, -1)

    return sent, rest


def per_device(
    table,
    request_rows,
    send_counts,
    lookup_owner,
    lookup_rank,
    bag_lengths,
    labels,
    w_first,
    w_second,
    w_out,
):
    peers = lax.axis_size(AXES)
    core_bit = lax.axis_size("gy").bit_length() - 1
    slots = request_rows.shape[2]
    width = table.shape[1]
    looks = lookup_owner.shape[0]
    samples = labels.shape[0]
    bags = bag_lengths.shape[1]
    inputs = w_first.shape[0]
    most = 8
    incoming = lax.all_to_all(
        request_rows, AXES, split_axis=1, concat_axis=0, tiled=True
    ).reshape(peers * slots)
    served = table[incoming]

    owner_ids = jnp.arange(peers, dtype=jnp.int32)
    match = lookup_owner[:, None] == owner_ids[None, :]
    lookup_count = jnp.sum(jnp.where(match, send_counts[0][None, :], 0), axis=1)
    slot = lookup_rank % lookup_count
    lengths = bag_lengths[0]
    starts = jnp.cumsum(lengths) - lengths
    scale = lax.rsqrt(lengths.astype(jnp.float32))[:, None]
    owner_pad = jnp.pad(lookup_owner, (0, most)).astype(jnp.bfloat16)
    slot_pad = jnp.pad(slot, (0, most)).astype(jnp.bfloat16)
    shifted = jnp.stack(
        [owner_pad[j : j + looks] for j in range(most)]
        + [slot_pad[j : j + looks] for j in range(most)]
    )
    served, shifted = lax.optimization_barrier((served, shifted))
    fetched = lax.all_to_all(
        served.reshape(peers, 1, slots, width), AXES, split_axis=0, concat_axis=1, tiled=True
    ).reshape(peers * slots, width)
    first = (starts[:, None] == jnp.arange(looks, dtype=jnp.int32)[None, :]).astype(jnp.bfloat16)
    found = lax.dot_general(
        first, shifted, (((1,), (1,)), ((), ())), preferred_element_type=jnp.float32
    )
    code = found[:, :most] * slots + found[:, most:]
    place = jnp.arange(most, dtype=jnp.int32)[None, :]
    code = jnp.where(place < lengths[:, None], code, -1.0)
    names = jnp.arange(peers * slots, dtype=jnp.int32).astype(jnp.float32)[None, :]
    counted = jnp.zeros((bags, peers * slots), jnp.float32)
    for j in range(most):
        counted = counted + (code[:, j : j + 1] == names).astype(jnp.float32)
    counted = lax.optimization_barrier(counted.astype(jnp.bfloat16))

    pooled = jnp.dot(counted, fetched, preferred_element_type=jnp.float32)
    x = (pooled * scale).astype(jnp.bfloat16).reshape(samples, inputs)
    x_left = gather_left(x, core_bit, core_bit + 1)
    z1 = jnp.dot(x, w_first, preferred_element_type=jnp.float32)
    h1 = jax.nn.silu(z1).astype(jnp.bfloat16)
    h1_left = gather_left(h1, core_bit, 0)
    z2 = jnp.dot(h1, w_second, preferred_element_type=jnp.float32)
    h2 = jax.nn.silu(z2).astype(jnp.bfloat16)
    logit = jnp.dot(h2, w_out, preferred_element_type=jnp.float32)
    dlogit = jax.nn.sigmoid(logit) - labels.astype(jnp.float32)
    dz2 = (dlogit[:, None] * w_out.astype(jnp.float32)[None, :] * silu_slope(z2)).astype(
        jnp.bfloat16
    )
    head_term = jnp.sum(dlogit[:, None] * h2.astype(jnp.float32), axis=0)
    dz2_all = gather_right(dz2, core_bit, 0)
    back_two = lax.dot_general(
        dz2, w_second, (((1,), (1,)), ((), ())), preferred_element_type=jnp.float32
    )
    dz1 = (back_two * silu_slope(z1)).astype(jnp.bfloat16)
    dz1_all = gather_right(dz1, core_bit, core_bit + 1)
    sent, second = halving(h1_left, dz2_all, core_bit, 0)
    sent, dz1 = lax.optimization_barrier((sent, dz1))
    grad_second = second(sent)
    sent, first = halving(x_left, dz1_all, core_bit, core_bit + 1)
    grad_first = first(sent)
    back_one = lax.dot_general(
        dz1, w_first, (((1,), (1,)), ((), ())), preferred_element_type=jnp.float32
    )
    bag_grad = (back_one.reshape(bags, width) * scale).astype(jnp.bfloat16)
    slot_grad = lax.dot_general(
        counted, bag_grad, (((0,), (0,)), ((), ())), preferred_element_type=jnp.float32
    )
    share = head_term.shape[0] // peers
    extra = -(-share // width)
    head = jnp.pad(head_term.reshape(peers, share), ((0, 0), (0, extra * width - share)))
    outgoing = jnp.concatenate(
        [slot_grad.reshape(peers, slots, width), head.reshape(peers, extra, width)], axis=1
    ).astype(jnp.bfloat16)
    returned = lax.all_to_all(outgoing[None], AXES, split_axis=1, concat_axis=0, tiled=True)[:, 0]
    grad_out = jnp.sum(returned[:, slots:].astype(jnp.float32), axis=0).reshape(-1)[:share]
    home = (
        jnp.arange(table.shape[0], dtype=jnp.int32)[:, None] == incoming[None, :]
    ).astype(jnp.bfloat16)
    row_grad = jnp.dot(
        home, returned[:, :slots].reshape(peers * slots, width), preferred_element_type=jnp.float32
    )
    return (grad_first, grad_second, grad_out, row_grad)


def solution(mesh):
    in_specs = (
        P(AXES, None),
        P(AXES, None, None),
        P(AXES, None),
        P(AXES),
        P(AXES),
        P(AXES, None),
        P(AXES),
        P(),
        P(),
        P(),
    )
    out_specs = (P(AXES, None), P(AXES, None), P(AXES), P(AXES, None))
    return jax.shard_map(
        per_device, mesh=mesh, in_specs=in_specs, out_specs=out_specs, check_vma=False
    )
```

```python
import functools

import jax
import jax.numpy as jnp
from jax import lax
from jax.experimental import pallas as pl
from jax.experimental.pallas import tpu as pltpu
from jax.sharding import PartitionSpec as P

AXES = ("gx", "gy")


def silu_slope(value):
    sig = jax.nn.sigmoid(value)
    return sig * (1.0 + value * (1.0 - sig))


def swap(value, mask):
    peers = lax.axis_size(AXES)
    return lax.ppermute(value, AXES, [(d, d ^ mask) for d in range(peers)])


def pick(value, dim, index):
    return lax.dynamic_index_in_dim(value, index, dim, keepdims=False)


def group(core_bit, side):
    core, near = 1 << core_bit, 1 << side
    return core, near, (lax.axis_index(AXES) >> core_bit) & 1, (lax.axis_index(AXES) >> side) & 1


def gather_left(left, core_bit, side):
    peers = lax.axis_size(AXES)
    core, near, my_core, my_near = group(core_bit, side)
    samples, total = left.shape
    bits = peers.bit_length() - 1
    one, two = bits - 1 - max(core_bit, side), bits - 1 - min(core_bit, side)
    split = left.T.reshape(
        1 << one, 2, 1 << (two - one - 1), 2, 1 << (bits - 1 - two), total // peers, samples
    )

    def quarter(c, n):
        outer, inner = (c, n) if core_bit > side else (n, c)
        return pick(pick(split, 3, inner), 1, outer)

    return jnp.concatenate(
        [
            quarter(my_core, my_near),
            swap(quarter(1 - my_core, my_near), core),
            swap(quarter(my_core, 1 - my_near), near),
            swap(quarter(1 - my_core, 1 - my_near), core + near),
        ],
        axis=-1,
    )


def gather_right(right, core_bit, side):
    core, near, _, _ = group(core_bit, side)
    across = swap(right, near)
    return jnp.concatenate([right, swap(right, core), across, swap(across, core)], axis=0)


def orders(peers, core_bit):
    bits = [b for b in range(peers.bit_length() - 1) if b != core_bit]
    high = [b for b in bits if b > core_bit]
    low = [b for b in bits if 0 < b < core_bit]
    return (high + low, [0] + high[1:] + low)


def arrange(left, core_bit, side, order):
    peers = lax.axis_size(AXES)
    bits = [b for b in range(peers.bit_length() - 2, -1, -1) if b not in (core_bit, side)]
    rows, depth = left.shape[-2:]
    left = left.reshape([2] * len(bits) + [rows, depth])
    left = left.transpose([bits.index(b) for b in order] + [len(bits), len(bits) + 1])
    return left.reshape(-1, depth)


def flip(bit, core_bit):
    gx, gy = lax.axis_index("gx"), lax.axis_index("gy")
    if bit < core_bit:
        mine = (gy // (1 << bit)) % 2
        return mine, (gx, gy + (1 - 2 * mine) * (1 << bit))
    up = 1 << (bit - core_bit)
    mine = (gx // up) % 2
    return mine, (gx + (1 - 2 * mine) * up, gy)


def halving_kernel(core_bit, both, l2, r2, l1, r1, o2, o1, *scratch):
    send_sem, recv_sem = scratch[-2:]
    steps = len(both[0])
    per = 3 * steps
    lefts, rights, outs = (l2, l1), (r2, r1), (o2, o1)
    accs = [scratch[g * per : g * per + steps] for g in range(2)]
    sends = [scratch[g * per + steps : g * per + 2 * steps] for g in range(2)]
    recvs = [scratch[g * per + 2 * steps : g * per + 3 * steps] for g in range(2)]
    chunks, _, wide = sends[0][0].shape
    union = sorted(set(both[0]) | set(both[1]))
    barrier = pltpu.get_barrier_semaphore()
    for bit in union:
        pl.semaphore_signal(
            barrier, inc=1, device_id=flip(bit, core_bit)[1], device_id_type=pl.DeviceIdType.MESH
        )
    pl.semaphore_wait(barrier, len(union))

    def copy(g, k, c):
        return pltpu.make_async_remote_copy(
            src_ref=sends[g][k].at[c],
            dst_ref=recvs[g][k].at[c],
            send_sem=send_sem.at[g, k, c],
            recv_sem=recv_sem.at[g, k, c],
            device_id=flip(both[g][k], core_bit)[1],
            device_id_type=pl.DeviceIdType.MESH,
        )

    def product(g, c, part):
        half = lefts[g].shape[0] // 2
        rows = lefts[g][pl.ds(pl.multiple_of(part * half, half), half), :]
        return jnp.dot(
            rows, rights[g][:, c * wide : (c + 1) * wide], preferred_element_type=jnp.float32
        )

    for c in range(chunks):
        for g in range(2):
            mine = flip(both[g][0], core_bit)[0]
            sends[g][0][c] = product(g, c, 1 - mine).astype(jnp.bfloat16)
            copy(g, 0, c).start()
    for c in range(chunks):
        for g in range(2):
            mine = flip(both[g][0], core_bit)[0]
            accs[g][0][c] = product(g, c, mine)
    for k in range(1, steps + 1):
        for c in range(chunks):
            for g in range(2):
                copy(g, k - 1, c).wait_recv()
                if k == steps:
                    outs[g][:, c * wide : (c + 1) * wide] = accs[g][k - 1][c] + recvs[g][k - 1][
                        c
                    ].astype(jnp.float32)
                    continue
                mine = flip(both[g][k], core_bit)[0]
                half = sends[g][k].shape[1]

                def total(part):
                    at = pl.ds(pl.multiple_of(part * half, half), half)
                    return accs[g][k - 1][c, at, :] + recvs[g][k - 1][c, at, :].astype(jnp.float32)

                sends[g][k][c] = total(1 - mine).astype(jnp.bfloat16)
                copy(g, k, c).start()
                accs[g][k][c] = total(mine)
    for k in range(steps):
        for c in range(chunks):
            for g in range(2):
                copy(g, k, c).wait_send()


def halve(l2, r2, l1, r1, core_bit, both):
    steps, chunks = len(both[0]), 2
    rows, depth = l2.shape
    columns = r2.shape[1]
    wide = columns // chunks
    scratch = []
    for _ in range(2):
        for kind in (jnp.float32, jnp.bfloat16, jnp.bfloat16):
            scratch += [pltpu.VMEM((chunks, rows >> (k + 1), wide), kind) for k in range(steps)]
    scratch += [pltpu.SemaphoreType.DMA((2, steps, chunks))] * 2
    whole = pl.BlockSpec(memory_space=pltpu.VMEM)
    out = jax.ShapeDtypeStruct((rows >> steps, columns), jnp.float32)
    return pl.pallas_call(
        functools.partial(halving_kernel, core_bit, both),
        out_shape=(out, out),
        in_specs=[whole] * 4,
        out_specs=(whole, whole),
        scratch_shapes=scratch,
        compiler_params=pltpu.CompilerParams(
            collective_id=0, has_side_effects=True, vmem_limit_bytes=40 << 20
        ),
        cost_estimate=pl.CostEstimate(
            flops=4 * rows * depth * columns,
            bytes_accessed=2 * (rows * depth + depth * columns) * 2,
            transcendentals=0,
        ),
    )(l2, r2, l1, r1)


def per_device(
    table,
    request_rows,
    send_counts,
    lookup_owner,
    lookup_rank,
    bag_lengths,
    labels,
    w_first,
    w_second,
    w_out,
):
    peers = lax.axis_size(AXES)
    core_bit = lax.axis_size("gy").bit_length() - 1
    slots = request_rows.shape[2]
    width = table.shape[1]
    looks = lookup_owner.shape[0]
    samples = labels.shape[0]
    bags = bag_lengths.shape[1]
    inputs = w_first.shape[0]
    most = 8
    incoming = lax.all_to_all(
        request_rows, AXES, split_axis=1, concat_axis=0, tiled=True
    ).reshape(peers * slots)
    served = table[incoming]

    owner_ids = jnp.arange(peers, dtype=jnp.int32)
    match = lookup_owner[:, None] == owner_ids[None, :]
    lookup_count = jnp.sum(jnp.where(match, send_counts[0][None, :], 0), axis=1)
    slot = lookup_rank % lookup_count
    lengths = bag_lengths[0]
    starts = jnp.cumsum(lengths) - lengths
    scale = lax.rsqrt(lengths.astype(jnp.float32))[:, None]
    owner_pad = jnp.pad(lookup_owner, (0, most)).astype(jnp.bfloat16)
    slot_pad = jnp.pad(slot, (0, most)).astype(jnp.bfloat16)
    shifted = jnp.stack(
        [owner_pad[j : j + looks] for j in range(most)]
        + [slot_pad[j : j + looks] for j in range(most)]
    )
    served, shifted = lax.optimization_barrier((served, shifted))
    fetched = lax.all_to_all(
        served.reshape(peers, 1, slots, width), AXES, split_axis=0, concat_axis=1, tiled=True
    ).reshape(peers * slots, width)
    first = (starts[:, None] == jnp.arange(looks, dtype=jnp.int32)[None, :]).astype(jnp.bfloat16)
    found = lax.dot_general(
        first, shifted, (((1,), (1,)), ((), ())), preferred_element_type=jnp.float32
    )
    code = found[:, :most] * slots + found[:, most:]
    place = jnp.arange(most, dtype=jnp.int32)[None, :]
    code = jnp.where(place < lengths[:, None], code, -1.0)
    names = jnp.arange(peers * slots, dtype=jnp.int32).astype(jnp.float32)[None, :]
    counted = jnp.zeros((bags, peers * slots), jnp.float32)
    for j in range(most):
        counted = counted + (code[:, j : j + 1] == names).astype(jnp.float32)
    counted = lax.optimization_barrier(counted.astype(jnp.bfloat16))

    pooled = jnp.dot(counted, fetched, preferred_element_type=jnp.float32)
    x = (pooled * scale).astype(jnp.bfloat16).reshape(samples, inputs)
    both = orders(peers, core_bit)
    x_left = arrange(gather_left(x, core_bit, core_bit + 1), core_bit, core_bit + 1, both[1])
    z1 = jnp.dot(x, w_first, preferred_element_type=jnp.float32)
    h1 = jax.nn.silu(z1).astype(jnp.bfloat16)
    x_left, h1 = lax.optimization_barrier((x_left, h1))
    h1_left = arrange(gather_left(h1, core_bit, 0), core_bit, 0, both[0])
    z2 = jnp.dot(h1, w_second, preferred_element_type=jnp.float32)
    h2 = jax.nn.silu(z2).astype(jnp.bfloat16)
    logit = jnp.dot(h2, w_out, preferred_element_type=jnp.float32)
    dlogit = jax.nn.sigmoid(logit) - labels.astype(jnp.float32)
    dz2 = (dlogit[:, None] * w_out.astype(jnp.float32)[None, :] * silu_slope(z2)).astype(
        jnp.bfloat16
    )
    h1_left, dz2 = lax.optimization_barrier((h1_left, dz2))
    head_term = jnp.sum(dlogit[:, None] * h2.astype(jnp.float32), axis=0)
    dz2_all = gather_right(dz2, core_bit, 0)
    back_two = lax.dot_general(
        dz2, w_second, (((1,), (1,)), ((), ())), preferred_element_type=jnp.float32
    )
    dz1 = (back_two * silu_slope(z1)).astype(jnp.bfloat16)
    dz1_all = gather_right(dz1, core_bit, core_bit + 1)
    grad_second, grad_first = halve(h1_left, dz2_all, x_left, dz1_all, core_bit, both)
    back_one = lax.dot_general(
        dz1, w_first, (((1,), (1,)), ((), ())), preferred_element_type=jnp.float32
    )
    bag_grad = (back_one.reshape(bags, width) * scale).astype(jnp.bfloat16)
    slot_grad = lax.dot_general(
        counted, bag_grad, (((0,), (0,)), ((), ())), preferred_element_type=jnp.float32
    )
    share = head_term.shape[0] // peers
    extra = -(-share // width)
    head = jnp.pad(head_term.reshape(peers, share), ((0, 0), (0, extra * width - share)))
    outgoing = jnp.concatenate(
        [slot_grad.reshape(peers, slots, width), head.reshape(peers, extra, width)], axis=1
    ).astype(jnp.bfloat16)
    returned = lax.all_to_all(outgoing[None], AXES, split_axis=1, concat_axis=0, tiled=True)[:, 0]
    grad_out = jnp.sum(returned[:, slots:].astype(jnp.float32), axis=0).reshape(-1)[:share]
    home = (
        jnp.arange(table.shape[0], dtype=jnp.int32)[:, None] == incoming[None, :]
    ).astype(jnp.bfloat16)
    row_grad = jnp.dot(
        home, returned[:, :slots].reshape(peers * slots, width), preferred_element_type=jnp.float32
    )
    return (grad_first, grad_second, grad_out, row_grad)


def solution(mesh):
    in_specs = (
        P(AXES, None),
        P(AXES, None, None),
        P(AXES, None),
        P(AXES),
        P(AXES),
        P(AXES, None),
        P(AXES),
        P(),
        P(),
        P(),
    )
    out_specs = (P(AXES, None), P(AXES, None), P(AXES), P(AXES, None))
    return jax.shard_map(
        per_device, mesh=mesh, in_specs=in_specs, out_specs=out_specs, check_vma=False
    )
```

```python
import functools

import jax
import jax.numpy as jnp
from jax import lax
from jax.experimental import pallas as pl
from jax.experimental.pallas import tpu as pltpu
from jax.sharding import PartitionSpec as P

AXES = ("gx", "gy")


def silu_slope(value):
    sig = jax.nn.sigmoid(value)
    return sig * (1.0 + value * (1.0 - sig))


def swap(value, mask):
    peers = lax.axis_size(AXES)
    return lax.ppermute(value, AXES, [(d, d ^ mask) for d in range(peers)])


def pick(value, dim, index):
    return lax.dynamic_index_in_dim(value, index, dim, keepdims=False)


def group(core_bit, side):
    core, near = 1 << core_bit, 1 << side
    return core, near, (lax.axis_index(AXES) >> core_bit) & 1, (lax.axis_index(AXES) >> side) & 1


def gather_left(left, core_bit, side):
    peers = lax.axis_size(AXES)
    core, near, my_core, my_near = group(core_bit, side)
    samples, total = left.shape
    bits = peers.bit_length() - 1
    one, two = bits - 1 - max(core_bit, side), bits - 1 - min(core_bit, side)
    split = left.T.reshape(
        1 << one, 2, 1 << (two - one - 1), 2, 1 << (bits - 1 - two), total // peers, samples
    )

    def quarter(c, n):
        outer, inner = (c, n) if core_bit > side else (n, c)
        return pick(pick(split, 3, inner), 1, outer)

    return jnp.concatenate(
        [
            quarter(my_core, my_near),
            swap(quarter(1 - my_core, my_near), core),
            swap(quarter(my_core, 1 - my_near), near),
            swap(quarter(1 - my_core, 1 - my_near), core + near),
        ],
        axis=-1,
    )


def gather_right(right, core_bit, side):
    core, near, _, _ = group(core_bit, side)
    across = swap(right, near)
    return jnp.concatenate([right, swap(right, core), across, swap(across, core)], axis=0)


def orders(peers, core_bit):
    bits = [b for b in range(peers.bit_length() - 1) if b != core_bit]
    high = [b for b in bits if b > core_bit]
    low = [b for b in bits if 0 < b < core_bit]
    return (high + low, [0] + high[1:] + low)


def arrange(left, core_bit, side, order):
    peers = lax.axis_size(AXES)
    bits = [b for b in range(peers.bit_length() - 2, -1, -1) if b not in (core_bit, side)]
    rows, depth = left.shape[-2:]
    left = left.reshape([2] * len(bits) + [rows, depth])
    left = left.transpose([bits.index(b) for b in order] + [len(bits), len(bits) + 1])
    return left.reshape(-1, depth)


def flip(bit, core_bit):
    gx, gy = lax.axis_index("gx"), lax.axis_index("gy")
    if bit < core_bit:
        mine = (gy // (1 << bit)) % 2
        return mine, (gx, gy + (1 - 2 * mine) * (1 << bit))
    up = 1 << (bit - core_bit)
    mine = (gx // up) % 2
    return mine, (gx + (1 - 2 * mine) * up, gy)


def halving_kernel(core_bit, both, l2, r2, l1, r1, o2, o1, *scratch):
    send_sem, recv_sem = scratch[-2:]
    steps = len(both[0])
    per = 3 * steps
    lefts, rights, outs = (l2, l1), (r2, r1), (o2, o1)
    accs = [scratch[g * per : g * per + steps] for g in range(2)]
    sends = [scratch[g * per + steps : g * per + 2 * steps] for g in range(2)]
    recvs = [scratch[g * per + 2 * steps : g * per + 3 * steps] for g in range(2)]
    chunks, _, wide = sends[0][0].shape
    union = sorted(set(both[0]) | set(both[1]))
    barrier = pltpu.get_barrier_semaphore()
    for bit in union:
        pl.semaphore_signal(
            barrier, inc=1, device_id=flip(bit, core_bit)[1], device_id_type=pl.DeviceIdType.MESH
        )
    pl.semaphore_wait(barrier, len(union))

    def copy(g, k, c):
        return pltpu.make_async_remote_copy(
            src_ref=sends[g][k].at[c],
            dst_ref=recvs[g][k].at[c],
            send_sem=send_sem.at[g, k, c],
            recv_sem=recv_sem.at[g, k, c],
            device_id=flip(both[g][k], core_bit)[1],
            device_id_type=pl.DeviceIdType.MESH,
        )

    def product(g, c, part):
        half = lefts[g].shape[0] // 2
        rows = lefts[g][pl.ds(pl.multiple_of(part * half, half), half), :]
        return jnp.dot(
            rows, rights[g][:, c * wide : (c + 1) * wide], preferred_element_type=jnp.float32
        )

    for c in range(chunks):
        for g in range(2):
            mine = flip(both[g][0], core_bit)[0]
            sends[g][0][c] = product(g, c, 1 - mine).astype(jnp.bfloat16)
            copy(g, 0, c).start()
    for c in range(chunks):
        for g in range(2):
            mine = flip(both[g][0], core_bit)[0]
            accs[g][0][c] = product(g, c, mine)
    for k in range(1, steps + 1):
        for c in range(chunks):
            for g in range(2):
                copy(g, k - 1, c).wait_recv()
                if k == steps:
                    outs[g][:, c * wide : (c + 1) * wide] = accs[g][k - 1][c] + recvs[g][k - 1][
                        c
                    ].astype(jnp.float32)
                    continue
                mine = flip(both[g][k], core_bit)[0]
                half = sends[g][k].shape[1]

                def total(part):
                    at = pl.ds(pl.multiple_of(part * half, half), half)
                    return accs[g][k - 1][c, at, :] + recvs[g][k - 1][c, at, :].astype(jnp.float32)

                sends[g][k][c] = total(1 - mine).astype(jnp.bfloat16)
                copy(g, k, c).start()
                accs[g][k][c] = total(mine)
    for k in range(steps):
        for c in range(chunks):
            for g in range(2):
                copy(g, k, c).wait_send()


def halve(l2, r2, l1, r1, core_bit, both):
    steps, chunks = len(both[0]), 4
    rows, depth = l2.shape
    columns = r2.shape[1]
    wide = columns // chunks
    scratch = []
    for _ in range(2):
        for kind in (jnp.float32, jnp.bfloat16, jnp.bfloat16):
            scratch += [pltpu.VMEM((chunks, rows >> (k + 1), wide), kind) for k in range(steps)]
    scratch += [pltpu.SemaphoreType.DMA((2, steps, chunks))] * 2
    whole = pl.BlockSpec(memory_space=pltpu.VMEM)
    out = jax.ShapeDtypeStruct((rows >> steps, columns), jnp.float32)
    return pl.pallas_call(
        functools.partial(halving_kernel, core_bit, both),
        out_shape=(out, out),
        in_specs=[whole] * 4,
        out_specs=(whole, whole),
        scratch_shapes=scratch,
        compiler_params=pltpu.CompilerParams(
            collective_id=0, has_side_effects=True, vmem_limit_bytes=40 << 20
        ),
        cost_estimate=pl.CostEstimate(
            flops=4 * rows * depth * columns,
            bytes_accessed=2 * (rows * depth + depth * columns) * 2,
            transcendentals=0,
        ),
    )(l2, r2, l1, r1)


def per_device(
    table,
    request_rows,
    send_counts,
    lookup_owner,
    lookup_rank,
    bag_lengths,
    labels,
    w_first,
    w_second,
    w_out,
):
    peers = lax.axis_size(AXES)
    core_bit = lax.axis_size("gy").bit_length() - 1
    slots = request_rows.shape[2]
    width = table.shape[1]
    looks = lookup_owner.shape[0]
    samples = labels.shape[0]
    bags = bag_lengths.shape[1]
    inputs = w_first.shape[0]
    most = 8
    incoming = lax.all_to_all(
        request_rows, AXES, split_axis=1, concat_axis=0, tiled=True
    ).reshape(peers * slots)
    home = (
        jnp.arange(table.shape[0], dtype=jnp.int32)[:, None] == incoming[None, :]
    ).astype(jnp.bfloat16)
    served = lax.dot_general(
        home, table, (((0,), (0,)), ((), ())), preferred_element_type=jnp.float32
    ).astype(jnp.bfloat16)

    owner_ids = jnp.arange(peers, dtype=jnp.int32)
    match = lookup_owner[:, None] == owner_ids[None, :]
    lookup_count = jnp.sum(jnp.where(match, send_counts[0][None, :], 0), axis=1)
    slot = lookup_rank % lookup_count
    lengths = bag_lengths[0]
    starts = jnp.cumsum(lengths) - lengths
    scale = lax.rsqrt(lengths.astype(jnp.float32))[:, None]
    owner_pad = jnp.pad(lookup_owner, (0, most)).astype(jnp.bfloat16)
    slot_pad = jnp.pad(slot, (0, most)).astype(jnp.bfloat16)
    shifted = jnp.stack(
        [owner_pad[j : j + looks] for j in range(most)]
        + [slot_pad[j : j + looks] for j in range(most)]
    )
    served, shifted = lax.optimization_barrier((served, shifted))
    fetched = lax.all_to_all(
        served.reshape(peers, 1, slots, width), AXES, split_axis=0, concat_axis=1, tiled=True
    ).reshape(peers * slots, width)
    first = (starts[:, None] == jnp.arange(looks, dtype=jnp.int32)[None, :]).astype(jnp.bfloat16)
    found = lax.dot_general(
        first, shifted, (((1,), (1,)), ((), ())), preferred_element_type=jnp.float32
    )
    code = found[:, :most] * slots + found[:, most:]
    place = jnp.arange(most, dtype=jnp.int32)[None, :]
    code = jnp.where(place < lengths[:, None], code, -1.0)
    names = jnp.arange(peers * slots, dtype=jnp.int32).astype(jnp.float32)[None, :]
    counted = jnp.zeros((bags, peers * slots), jnp.float32)
    for j in range(most):
        counted = counted + (code[:, j : j + 1] == names).astype(jnp.float32)
    counted = lax.optimization_barrier(counted.astype(jnp.bfloat16))

    pooled = jnp.dot(counted, fetched, preferred_element_type=jnp.float32)
    x = (pooled * scale).astype(jnp.bfloat16).reshape(samples, inputs)
    both = orders(peers, core_bit)
    x_left = arrange(gather_left(x, core_bit, core_bit + 1), core_bit, core_bit + 1, both[1])
    z1 = jnp.dot(x, w_first, preferred_element_type=jnp.float32)
    h1 = jax.nn.silu(z1).astype(jnp.bfloat16)
    x_left, h1 = lax.optimization_barrier((x_left, h1))
    h1_left = arrange(gather_left(h1, core_bit, 0), core_bit, 0, both[0])
    z2 = jnp.dot(h1, w_second, preferred_element_type=jnp.float32)
    h2 = jax.nn.silu(z2).astype(jnp.bfloat16)
    logit = jnp.dot(h2, w_out, preferred_element_type=jnp.float32)
    dlogit = jax.nn.sigmoid(logit) - labels.astype(jnp.float32)
    dz2 = (dlogit[:, None] * w_out.astype(jnp.float32)[None, :] * silu_slope(z2)).astype(
        jnp.bfloat16
    )
    head_term = jnp.sum(dlogit[:, None] * h2.astype(jnp.float32), axis=0)
    dz2_all = gather_right(dz2, core_bit, 0)
    back_two = lax.dot_general(
        dz2, w_second, (((1,), (1,)), ((), ())), preferred_element_type=jnp.float32
    )
    dz1 = (back_two * silu_slope(z1)).astype(jnp.bfloat16)
    h1_left, dz1 = lax.optimization_barrier((h1_left, dz1))
    dz1_all = gather_right(dz1, core_bit, core_bit + 1)
    back_one = lax.dot_general(
        dz1, w_first, (((1,), (1,)), ((), ())), preferred_element_type=jnp.float32
    )
    bag_grad = (back_one.reshape(bags, width) * scale).astype(jnp.bfloat16)
    slot_grad = lax.dot_general(
        counted, bag_grad, (((0,), (0,)), ((), ())), preferred_element_type=jnp.float32
    )
    share = head_term.shape[0] // peers
    extra = -(-share // width)
    head = jnp.pad(head_term.reshape(peers, share), ((0, 0), (0, extra * width - share)))
    outgoing = jnp.concatenate(
        [slot_grad.reshape(peers, slots, width), head.reshape(peers, extra, width)], axis=1
    ).astype(jnp.bfloat16)
    outgoing, dz1_all = lax.optimization_barrier((outgoing, dz1_all))
    returned = lax.all_to_all(outgoing[None], AXES, split_axis=1, concat_axis=0, tiled=True)[:, 0]
    grad_second, grad_first = halve(h1_left, dz2_all, x_left, dz1_all, core_bit, both)
    grad_out = jnp.sum(returned[:, slots:].astype(jnp.float32), axis=0).reshape(-1)[:share]
    row_grad = jnp.dot(
        home, returned[:, :slots].reshape(peers * slots, width), preferred_element_type=jnp.float32
    )
    return (grad_first, grad_second, grad_out, row_grad)


def solution(mesh):
    in_specs = (
        P(AXES, None),
        P(AXES, None, None),
        P(AXES, None),
        P(AXES),
        P(AXES),
        P(AXES, None),
        P(AXES),
        P(),
        P(),
        P(),
    )
    out_specs = (P(AXES, None), P(AXES, None), P(AXES), P(AXES, None))
    return jax.shard_map(
        per_device, mesh=mesh, in_specs=in_specs, out_specs=out_specs, check_vma=False
    )
```

```python
import functools

import jax
import jax.numpy as jnp
from jax import lax
from jax.experimental import pallas as pl
from jax.experimental.pallas import tpu as pltpu
from jax.sharding import PartitionSpec as P

AXES = ("gx", "gy")


def silu_slope(value):
    sig = jax.nn.sigmoid(value)
    return sig * (1.0 + value * (1.0 - sig))


def swap(value, mask):
    peers = lax.axis_size(AXES)
    return lax.ppermute(value, AXES, [(d, d ^ mask) for d in range(peers)])


def pick(value, dim, index):
    return lax.dynamic_index_in_dim(value, index, dim, keepdims=False)


def group(core_bit, side):
    core, near = 1 << core_bit, 1 << side
    return core, near, (lax.axis_index(AXES) >> core_bit) & 1, (lax.axis_index(AXES) >> side) & 1


def gather_left(left, core_bit, side):
    peers = lax.axis_size(AXES)
    core, near, my_core, my_near = group(core_bit, side)
    samples, total = left.shape
    bits = peers.bit_length() - 1
    one, two = bits - 1 - max(core_bit, side), bits - 1 - min(core_bit, side)
    split = left.T.reshape(
        1 << one, 2, 1 << (two - one - 1), 2, 1 << (bits - 1 - two), total // peers, samples
    )

    def quarter(c, n):
        outer, inner = (c, n) if core_bit > side else (n, c)
        return pick(pick(split, 3, inner), 1, outer)

    return jnp.concatenate(
        [
            quarter(my_core, my_near),
            swap(quarter(1 - my_core, my_near), core),
            swap(quarter(my_core, 1 - my_near), near),
            swap(quarter(1 - my_core, 1 - my_near), core + near),
        ],
        axis=-1,
    )


def gather_right(right, across, core_bit):
    core = 1 << core_bit
    return jnp.concatenate([right, swap(right, core), across, swap(across, core)], axis=0)


def orders(peers, core_bit):
    bits = [b for b in range(peers.bit_length() - 1) if b != core_bit]
    high = [b for b in bits if b > core_bit]
    low = [b for b in bits if 0 < b < core_bit]
    return (high + low, [0] + high[1:] + low)


def arrange(left, core_bit, side, order):
    peers = lax.axis_size(AXES)
    bits = [b for b in range(peers.bit_length() - 2, -1, -1) if b not in (core_bit, side)]
    rows, depth = left.shape[-2:]
    left = left.reshape([2] * len(bits) + [rows, depth])
    left = left.transpose([bits.index(b) for b in order] + [len(bits), len(bits) + 1])
    return left.reshape(-1, depth)


def flip(bit, core_bit):
    gx, gy = lax.axis_index("gx"), lax.axis_index("gy")
    if bit < core_bit:
        mine = (gy // (1 << bit)) % 2
        return mine, (gx, gy + (1 - 2 * mine) * (1 << bit))
    up = 1 << (bit - core_bit)
    mine = (gx // up) % 2
    return mine, (gx + (1 - 2 * mine) * up, gy)


def halving_kernel(core_bit, both, l2, r2, l1, r1, o2, o1, *scratch):
    send_sem, recv_sem = scratch[-2:]
    steps = len(both[0])
    per = 3 * steps
    lefts, rights, outs = (l2, l1), (r2, r1), (o2, o1)
    accs = [scratch[g * per : g * per + steps] for g in range(2)]
    sends = [scratch[g * per + steps : g * per + 2 * steps] for g in range(2)]
    recvs = [scratch[g * per + 2 * steps : g * per + 3 * steps] for g in range(2)]
    chunks, _, wide = sends[0][0].shape
    union = sorted(set(both[0]) | set(both[1]))
    barrier = pltpu.get_barrier_semaphore()
    for bit in union:
        pl.semaphore_signal(
            barrier, inc=1, device_id=flip(bit, core_bit)[1], device_id_type=pl.DeviceIdType.MESH
        )
    pl.semaphore_wait(barrier, len(union))

    def copy(g, k, c):
        return pltpu.make_async_remote_copy(
            src_ref=sends[g][k].at[c],
            dst_ref=recvs[g][k].at[c],
            send_sem=send_sem.at[g, k, c],
            recv_sem=recv_sem.at[g, k, c],
            device_id=flip(both[g][k], core_bit)[1],
            device_id_type=pl.DeviceIdType.MESH,
        )

    def product(g, c, part):
        half = lefts[g].shape[0] // 2
        rows = lefts[g][pl.ds(pl.multiple_of(part * half, half), half), :]
        return jnp.dot(
            rows, rights[g][:, c * wide : (c + 1) * wide], preferred_element_type=jnp.float32
        )

    for c in range(chunks):
        for g in range(2):
            mine = flip(both[g][0], core_bit)[0]
            sends[g][0][c] = product(g, c, 1 - mine).astype(jnp.bfloat16)
            copy(g, 0, c).start()
    for c in range(chunks):
        for g in range(2):
            mine = flip(both[g][0], core_bit)[0]
            accs[g][0][c] = product(g, c, mine)
    diagonal = [
        (k, t - k) for t in range(steps + chunks) for k in range(1, steps + 1) if 0 <= t - k < chunks
    ]
    for k, c in diagonal:
        for g in range(2):
            copy(g, k - 1, c).wait_recv()
            if k == steps:
                outs[g][:, c * wide : (c + 1) * wide] = accs[g][k - 1][c] + recvs[g][k - 1][
                    c
                ].astype(jnp.float32)
                continue
            mine = flip(both[g][k], core_bit)[0]
            half = sends[g][k].shape[1]

            def total(part):
                at = pl.ds(pl.multiple_of(part * half, half), half)
                return accs[g][k - 1][c, at, :] + recvs[g][k - 1][c, at, :].astype(jnp.float32)

            sends[g][k][c] = total(1 - mine).astype(jnp.bfloat16)
            copy(g, k, c).start()
            accs[g][k][c] = total(mine)
    for k in range(steps):
        for c in range(chunks):
            for g in range(2):
                copy(g, k, c).wait_send()


def halve(l2, r2, l1, r1, core_bit, both):
    steps, chunks = len(both[0]), 4
    rows, depth = l2.shape
    columns = r2.shape[1]
    wide = columns // chunks
    scratch = []
    for _ in range(2):
        for kind in (jnp.float32, jnp.bfloat16, jnp.bfloat16):
            scratch += [pltpu.VMEM((chunks, rows >> (k + 1), wide), kind) for k in range(steps)]
    scratch += [pltpu.SemaphoreType.DMA((2, steps, chunks))] * 2
    whole = pl.BlockSpec(memory_space=pltpu.VMEM)
    out = jax.ShapeDtypeStruct((rows >> steps, columns), jnp.float32)
    return pl.pallas_call(
        functools.partial(halving_kernel, core_bit, both),
        out_shape=(out, out),
        in_specs=[whole] * 4,
        out_specs=(whole, whole),
        scratch_shapes=scratch,
        compiler_params=pltpu.CompilerParams(
            collective_id=0, has_side_effects=True, vmem_limit_bytes=40 << 20
        ),
        cost_estimate=pl.CostEstimate(
            flops=4 * rows * depth * columns,
            bytes_accessed=2 * (rows * depth + depth * columns) * 2,
            transcendentals=0,
        ),
    )(l2, r2, l1, r1)


def per_device(
    table,
    request_rows,
    send_counts,
    lookup_owner,
    lookup_rank,
    bag_lengths,
    labels,
    w_first,
    w_second,
    w_out,
):
    peers = lax.axis_size(AXES)
    core_bit = lax.axis_size("gy").bit_length() - 1
    slots = request_rows.shape[2]
    width = table.shape[1]
    looks = lookup_owner.shape[0]
    samples = labels.shape[0]
    bags = bag_lengths.shape[1]
    inputs = w_first.shape[0]
    most = 8
    incoming = lax.all_to_all(
        request_rows, AXES, split_axis=1, concat_axis=0, tiled=True
    ).reshape(peers * slots)
    home = (
        jnp.arange(table.shape[0], dtype=jnp.int32)[:, None] == incoming[None, :]
    ).astype(jnp.bfloat16)
    served = lax.dot_general(
        home, table, (((0,), (0,)), ((), ())), preferred_element_type=jnp.float32
    ).astype(jnp.bfloat16)

    owner_ids = jnp.arange(peers, dtype=jnp.int32)
    match = lookup_owner[:, None] == owner_ids[None, :]
    lookup_count = jnp.sum(jnp.where(match, send_counts[0][None, :], 0), axis=1)
    slot = lookup_rank % lookup_count
    lengths = bag_lengths[0]
    starts = jnp.cumsum(lengths) - lengths
    scale = lax.rsqrt(lengths.astype(jnp.float32))[:, None]
    owner_pad = jnp.pad(lookup_owner, (0, most)).astype(jnp.bfloat16)
    slot_pad = jnp.pad(slot, (0, most)).astype(jnp.bfloat16)
    shifted = jnp.stack(
        [owner_pad[j : j + looks] for j in range(most)]
        + [slot_pad[j : j + looks] for j in range(most)]
    )
    served, shifted = lax.optimization_barrier((served, shifted))
    fetched = lax.all_to_all(
        served.reshape(peers, 1, slots, width), AXES, split_axis=0, concat_axis=1, tiled=True
    ).reshape(peers * slots, width)
    first = (starts[:, None] == jnp.arange(looks, dtype=jnp.int32)[None, :]).astype(jnp.bfloat16)
    found = lax.dot_general(
        first, shifted, (((1,), (1,)), ((), ())), preferred_element_type=jnp.float32
    )
    code = found[:, :most] * slots + found[:, most:]
    place = jnp.arange(most, dtype=jnp.int32)[None, :]
    code = jnp.where(place < lengths[:, None], code, -1.0)
    names = jnp.arange(peers * slots, dtype=jnp.int32).astype(jnp.float32)[None, :]
    counted = jnp.zeros((bags, peers * slots), jnp.float32)
    for j in range(most):
        counted = counted + (code[:, j : j + 1] == names).astype(jnp.float32)
    counted = lax.optimization_barrier(counted.astype(jnp.bfloat16))

    pooled = jnp.dot(counted, fetched, preferred_element_type=jnp.float32)
    x = (pooled * scale).astype(jnp.bfloat16).reshape(samples, inputs)
    both = orders(peers, core_bit)
    x_left = arrange(gather_left(x, core_bit, core_bit + 1), core_bit, core_bit + 1, both[1])
    z1 = jnp.dot(x, w_first, preferred_element_type=jnp.float32)
    h1 = jax.nn.silu(z1).astype(jnp.bfloat16)
    x_left, h1 = lax.optimization_barrier((x_left, h1))
    h1_left = arrange(gather_left(h1, core_bit, 0), core_bit, 0, both[0])
    z2 = jnp.dot(h1, w_second, preferred_element_type=jnp.float32)
    h2 = jax.nn.silu(z2).astype(jnp.bfloat16)
    logit = jnp.dot(h2, w_out, preferred_element_type=jnp.float32)
    dlogit = jax.nn.sigmoid(logit) - labels.astype(jnp.float32)
    dz2 = (dlogit[:, None] * w_out.astype(jnp.float32)[None, :] * silu_slope(z2)).astype(
        jnp.bfloat16
    )
    head_term = jnp.sum(dlogit[:, None] * h2.astype(jnp.float32), axis=0)
    across2 = swap(dz2, 1)
    back_two = lax.dot_general(
        dz2, w_second, (((1,), (1,)), ((), ())), preferred_element_type=jnp.float32
    )
    dz1 = (back_two * silu_slope(z1)).astype(jnp.bfloat16)
    h1_left, dz1 = lax.optimization_barrier((h1_left, dz1))
    across1 = swap(dz1, 2 << core_bit)
    back_one = lax.dot_general(
        dz1, w_first, (((1,), (1,)), ((), ())), preferred_element_type=jnp.float32
    )
    bag_grad = (back_one.reshape(bags, width) * scale).astype(jnp.bfloat16)
    across2, across1, bag_grad = lax.optimization_barrier((across2, across1, bag_grad))
    dz2_all = gather_right(dz2, across2, core_bit)
    dz1_all = gather_right(dz1, across1, core_bit)
    slot_grad = lax.dot_general(
        counted, bag_grad, (((0,), (0,)), ((), ())), preferred_element_type=jnp.float32
    )
    share = head_term.shape[0] // peers
    extra = -(-share // width)
    head = jnp.pad(head_term.reshape(peers, share), ((0, 0), (0, extra * width - share)))
    outgoing = jnp.concatenate(
        [slot_grad.reshape(peers, slots, width), head.reshape(peers, extra, width)], axis=1
    ).astype(jnp.bfloat16)
    outgoing, dz1_all = lax.optimization_barrier((outgoing, dz1_all))
    returned = lax.all_to_all(outgoing[None], AXES, split_axis=1, concat_axis=0, tiled=True)[:, 0]
    grad_second, grad_first = halve(h1_left, dz2_all, x_left, dz1_all, core_bit, both)
    grad_out = jnp.sum(returned[:, slots:].astype(jnp.float32), axis=0).reshape(-1)[:share]
    row_grad = jnp.dot(
        home, returned[:, :slots].reshape(peers * slots, width), preferred_element_type=jnp.float32
    )
    return (grad_first, grad_second, grad_out, row_grad)


def solution(mesh):
    in_specs = (
        P(AXES, None),
        P(AXES, None, None),
        P(AXES, None),
        P(AXES),
        P(AXES),
        P(AXES, None),
        P(AXES),
        P(),
        P(),
        P(),
    )
    out_specs = (P(AXES, None), P(AXES, None), P(AXES), P(AXES, None))
    return jax.shard_map(
        per_device, mesh=mesh, in_specs=in_specs, out_specs=out_specs, check_vma=False
    )
```

```python
import functools

import jax
import jax.numpy as jnp
from jax import lax
from jax.experimental import pallas as pl
from jax.experimental.pallas import tpu as pltpu
from jax.sharding import PartitionSpec as P

AXES = ("gx", "gy")


def silu_slope(value):
    sig = jax.nn.sigmoid(value)
    return sig * (1.0 + value * (1.0 - sig))


def swap(value, mask):
    peers = lax.axis_size(AXES)
    return lax.ppermute(value, AXES, [(d, d ^ mask) for d in range(peers)])


def pick(value, dim, index):
    return lax.dynamic_index_in_dim(value, index, dim, keepdims=False)


def group(core_bit, side):
    core, near = 1 << core_bit, 1 << side
    return core, near, (lax.axis_index(AXES) >> core_bit) & 1, (lax.axis_index(AXES) >> side) & 1


def gather_left(left, core_bit, side):
    peers = lax.axis_size(AXES)
    core, near, my_core, my_near = group(core_bit, side)
    samples, total = left.shape
    bits = peers.bit_length() - 1
    one, two = bits - 1 - max(core_bit, side), bits - 1 - min(core_bit, side)
    split = left.T.reshape(
        1 << one, 2, 1 << (two - one - 1), 2, 1 << (bits - 1 - two), total // peers, samples
    )

    def quarter(c, n):
        outer, inner = (c, n) if core_bit > side else (n, c)
        return pick(pick(split, 3, inner), 1, outer)

    return jnp.concatenate(
        [
            quarter(my_core, my_near),
            swap(quarter(1 - my_core, my_near), core),
            swap(quarter(my_core, 1 - my_near), near),
            swap(quarter(1 - my_core, 1 - my_near), core + near),
        ],
        axis=-1,
    )


def gather_right(right, across, core_bit):
    core = 1 << core_bit
    return jnp.concatenate([right, swap(right, core), across, swap(across, core)], axis=0)


def orders(peers, core_bit):
    bits = [b for b in range(peers.bit_length() - 1) if b != core_bit]
    high = [b for b in bits if b > core_bit]
    low = [b for b in bits if 0 < b < core_bit]
    return (high + low, [0] + high[1:] + low)


def arrange(left, core_bit, side, order):
    peers = lax.axis_size(AXES)
    bits = [b for b in range(peers.bit_length() - 2, -1, -1) if b not in (core_bit, side)]
    rows, depth = left.shape[-2:]
    left = left.reshape([2] * len(bits) + [rows, depth])
    left = left.transpose([bits.index(b) for b in order] + [len(bits), len(bits) + 1])
    return left.reshape(-1, depth)


def flip(bit, core_bit):
    gx, gy = lax.axis_index("gx"), lax.axis_index("gy")
    if bit < core_bit:
        mine = (gy // (1 << bit)) % 2
        return mine, (gx, gy + (1 - 2 * mine) * (1 << bit))
    up = 1 << (bit - core_bit)
    mine = (gx // up) % 2
    return mine, (gx + (1 - 2 * mine) * up, gy)


def halving_kernel(core_bit, both, l2, r2, l1, r1, o2, o1, *scratch):
    send_sem, recv_sem = scratch[-2:]
    steps = len(both[0])
    per = 3 * steps
    lefts, rights, outs = (l2, l1), (r2, r1), (o2, o1)
    accs = [scratch[g * per : g * per + steps] for g in range(2)]
    sends = [scratch[g * per + steps : g * per + 2 * steps] for g in range(2)]
    recvs = [scratch[g * per + 2 * steps : g * per + 3 * steps] for g in range(2)]
    chunks, _, wide = sends[0][0].shape
    union = sorted(set(both[0]) | set(both[1]))
    barrier = pltpu.get_barrier_semaphore()
    for bit in union:
        pl.semaphore_signal(
            barrier, inc=1, device_id=flip(bit, core_bit)[1], device_id_type=pl.DeviceIdType.MESH
        )
    pl.semaphore_wait(barrier, len(union))

    def copy(g, k, c):
        return pltpu.make_async_remote_copy(
            src_ref=sends[g][k].at[c],
            dst_ref=recvs[g][k].at[c],
            send_sem=send_sem.at[g, k, c],
            recv_sem=recv_sem.at[g, k, c],
            device_id=flip(both[g][k], core_bit)[1],
            device_id_type=pl.DeviceIdType.MESH,
        )

    def product(g, c, part):
        half = lefts[g].shape[0] // 2
        rows = lefts[g][pl.ds(pl.multiple_of(part * half, half), half), :]
        return jnp.dot(
            rows, rights[g][:, c * wide : (c + 1) * wide], preferred_element_type=jnp.float32
        )

    for c in range(chunks):
        for g in range(2):
            mine = flip(both[g][0], core_bit)[0]
            sends[g][0][c] = product(g, c, 1 - mine).astype(jnp.bfloat16)
            copy(g, 0, c).start()
    for c in range(chunks):
        for g in range(2):
            mine = flip(both[g][0], core_bit)[0]
            accs[g][0][c] = product(g, c, mine)
    diagonal = [
        (k, t - k) for t in range(steps + chunks) for k in range(1, steps + 1) if 0 <= t - k < chunks
    ]
    for k, c in diagonal:
        for g in range(2):
            copy(g, k - 1, c).wait_recv()
            if k == steps:
                outs[g][:, c * wide : (c + 1) * wide] = accs[g][k - 1][c] + recvs[g][k - 1][
                    c
                ].astype(jnp.float32)
                continue
            mine = flip(both[g][k], core_bit)[0]
            half = sends[g][k].shape[1]

            def total(part):
                at = pl.ds(pl.multiple_of(part * half, half), half)
                return accs[g][k - 1][c, at, :] + recvs[g][k - 1][c, at, :].astype(jnp.float32)

            sends[g][k][c] = total(1 - mine).astype(jnp.bfloat16)
            copy(g, k, c).start()
            accs[g][k][c] = total(mine)
    for k in range(steps):
        for c in range(chunks):
            for g in range(2):
                copy(g, k, c).wait_send()


def halve(l2, r2, l1, r1, core_bit, both):
    steps, chunks = len(both[0]), 4
    rows, depth = l2.shape
    columns = r2.shape[1]
    wide = columns // chunks
    scratch = []
    for _ in range(2):
        for kind in (jnp.float32, jnp.bfloat16, jnp.bfloat16):
            scratch += [pltpu.VMEM((chunks, rows >> (k + 1), wide), kind) for k in range(steps)]
    scratch += [pltpu.SemaphoreType.DMA((2, steps, chunks))] * 2
    whole = pl.BlockSpec(memory_space=pltpu.VMEM)
    out = jax.ShapeDtypeStruct((rows >> steps, columns), jnp.float32)
    return pl.pallas_call(
        functools.partial(halving_kernel, core_bit, both),
        out_shape=(out, out),
        in_specs=[whole] * 4,
        out_specs=(whole, whole),
        scratch_shapes=scratch,
        compiler_params=pltpu.CompilerParams(
            collective_id=0, has_side_effects=True, vmem_limit_bytes=40 << 20
        ),
        cost_estimate=pl.CostEstimate(
            flops=4 * rows * depth * columns,
            bytes_accessed=2 * (rows * depth + depth * columns) * 2,
            transcendentals=0,
        ),
    )(l2, r2, l1, r1)


def per_device(
    table,
    request_rows,
    send_counts,
    lookup_owner,
    lookup_rank,
    bag_lengths,
    labels,
    w_first,
    w_second,
    w_out,
):
    peers = lax.axis_size(AXES)
    core_bit = lax.axis_size("gy").bit_length() - 1
    slots = request_rows.shape[2]
    width = table.shape[1]
    looks = lookup_owner.shape[0]
    samples = labels.shape[0]
    bags = bag_lengths.shape[1]
    inputs = w_first.shape[0]
    most = 8
    incoming = lax.all_to_all(
        request_rows, AXES, split_axis=1, concat_axis=0, tiled=True
    ).reshape(peers * slots)
    home = (
        jnp.arange(table.shape[0], dtype=jnp.int32)[:, None] == incoming[None, :]
    ).astype(jnp.bfloat16)
    served = lax.dot_general(
        home, table, (((0,), (0,)), ((), ())), preferred_element_type=jnp.float32
    ).astype(jnp.bfloat16)

    owner_ids = jnp.arange(peers, dtype=jnp.int32)
    match = lookup_owner[:, None] == owner_ids[None, :]
    lookup_count = jnp.sum(jnp.where(match, send_counts[0][None, :], 0), axis=1)
    slot = lookup_rank % lookup_count
    lengths = bag_lengths[0]
    starts = jnp.cumsum(lengths) - lengths
    scale = lax.rsqrt(lengths.astype(jnp.float32))[:, None]
    owner_pad = jnp.pad(lookup_owner, (0, most)).astype(jnp.bfloat16)
    slot_pad = jnp.pad(slot, (0, most)).astype(jnp.bfloat16)
    shifted = jnp.stack(
        [owner_pad[j : j + looks] for j in range(most)]
        + [slot_pad[j : j + looks] for j in range(most)]
    )
    served, shifted = lax.optimization_barrier((served, shifted))
    fetched = lax.all_to_all(
        served.reshape(peers, 1, slots, width), AXES, split_axis=0, concat_axis=1, tiled=True
    ).reshape(peers * slots, width)
    first = (starts[:, None] == jnp.arange(looks, dtype=jnp.int32)[None, :]).astype(jnp.bfloat16)
    found = lax.dot_general(
        first, shifted, (((1,), (1,)), ((), ())), preferred_element_type=jnp.float32
    )
    code = found[:, :most] * slots + found[:, most:]
    place = jnp.arange(most, dtype=jnp.int32)[None, :]
    code = jnp.where(place < lengths[:, None], code, -1.0)
    names = jnp.arange(peers * slots, dtype=jnp.int32).astype(jnp.float32)[None, :]
    counted = jnp.zeros((bags, peers * slots), jnp.float32)
    for j in range(most):
        counted = counted + (code[:, j : j + 1] == names).astype(jnp.float32)
    counted = lax.optimization_barrier(counted.astype(jnp.bfloat16))

    pooled = jnp.dot(counted, fetched, preferred_element_type=jnp.float32)
    x = (pooled * scale).astype(jnp.bfloat16).reshape(samples, inputs)
    both = orders(peers, core_bit)
    x_left = arrange(gather_left(x, core_bit, core_bit + 1), core_bit, core_bit + 1, both[1])
    z1 = jnp.dot(x, w_first, preferred_element_type=jnp.float32)
    h1 = jax.nn.silu(z1).astype(jnp.bfloat16)
    x_left, h1 = lax.optimization_barrier((x_left, h1))
    h1_left = arrange(gather_left(h1, core_bit, 0), core_bit, 0, both[0])
    z2 = jnp.dot(h1, w_second, preferred_element_type=jnp.float32)
    h2 = jax.nn.silu(z2).astype(jnp.bfloat16)
    logit = jnp.dot(h2, w_out, preferred_element_type=jnp.float32)
    dlogit = jax.nn.sigmoid(logit) - labels.astype(jnp.float32)
    dz2 = (dlogit[:, None] * w_out.astype(jnp.float32)[None, :] * silu_slope(z2)).astype(
        jnp.bfloat16
    )
    head_term = jnp.sum(dlogit[:, None] * h2.astype(jnp.float32), axis=0)
    across2 = swap(dz2, 1)
    back_two = lax.dot_general(
        dz2, w_second, (((1,), (1,)), ((), ())), preferred_element_type=jnp.float32
    )
    dz1 = (back_two * silu_slope(z1)).astype(jnp.bfloat16)
    across1 = swap(dz1, 2 << core_bit)
    back_one = lax.dot_general(
        dz1, w_first, (((1,), (1,)), ((), ())), preferred_element_type=jnp.float32
    )
    bag_grad = (back_one.reshape(bags, width) * scale).astype(jnp.bfloat16)
    across2, across1, h1_left, bag_grad = lax.optimization_barrier(
        (across2, across1, h1_left, bag_grad)
    )
    dz2_all = gather_right(dz2, across2, core_bit)
    dz1_all = gather_right(dz1, across1, core_bit)
    slot_grad = lax.dot_general(
        counted, bag_grad, (((0,), (0,)), ((), ())), preferred_element_type=jnp.float32
    )
    share = head_term.shape[0] // peers
    extra = -(-share // width)
    head = jnp.pad(head_term.reshape(peers, share), ((0, 0), (0, extra * width - share)))
    outgoing = jnp.concatenate(
        [slot_grad.reshape(peers, slots, width), head.reshape(peers, extra, width)], axis=1
    ).astype(jnp.bfloat16)
    outgoing, dz1_all = lax.optimization_barrier((outgoing, dz1_all))
    returned = lax.all_to_all(outgoing[None], AXES, split_axis=1, concat_axis=0, tiled=True)[:, 0]
    grad_second, grad_first = halve(h1_left, dz2_all, x_left, dz1_all, core_bit, both)
    grad_out = jnp.sum(returned[:, slots:].astype(jnp.float32), axis=0).reshape(-1)[:share]
    row_grad = jnp.dot(
        home, returned[:, :slots].reshape(peers * slots, width), preferred_element_type=jnp.float32
    )
    return (grad_first, grad_second, grad_out, row_grad)


def solution(mesh):
    in_specs = (
        P(AXES, None),
        P(AXES, None, None),
        P(AXES, None),
        P(AXES),
        P(AXES),
        P(AXES, None),
        P(AXES),
        P(),
        P(),
        P(),
    )
    out_specs = (P(AXES, None), P(AXES, None), P(AXES), P(AXES, None))
    return jax.shard_map(
        per_device, mesh=mesh, in_specs=in_specs, out_specs=out_specs, check_vma=False
    )
```
